128 devices in a mesh: grp: 8 (over x, y_hi), in: 16 (over y_lo, z, core).
Axes of the slice: x: 4, y: 4 (y_hi: 2, y_lo: 2; y = y_hi * 2 + y_lo), z: 4, core: 2. Of those that a mesh axis runs over, the one named last changes fastest.
Arguments:
- view_one: float32 [32768, 256], P(('grp', 'in')), may hold values from -6 to 6
- view_two: float32 [32768, 256], P(('grp', 'in')), may hold values from -6 to 6
Outputs:
- loss: float32 [], replicated
- grad_one: float32 [32768, 256], P(('grp', 'in'))
- grad_two: float32 [32768, 256], P(('grp', 'in'))
The draws below stay inside these ranges and needn't reach their ends.
All inputs are finite; a program needn't handle non-finite values.
Results may differ from the reference program's by a relative error of at most 0.005.
Values may be sent and summed in bfloat16 or wider, within the bound.
A program may use at most 192 MiB of HBM per device.

```python
import jax
import jax.numpy as jnp
from jax import lax

D = 256
BATCH = 32768


def shared_rows(key):
    keys = jax.random.split(key, 3)
    cluster_ids = jax.random.randint(keys[0], (BATCH,), 0, 64)
    centers = jax.random.normal(keys[1], (64, D), jnp.float32)
    row_noise = jax.random.normal(keys[2], (BATCH, D), jnp.float32)
    return centers[cluster_ids] + row_noise


def rising_weight(low, high):
    position = jnp.arange(BATCH, dtype=jnp.float32)[:, None] / BATCH
    return low + (high - low) * position


def draw_view_one(key, part):
    base = shared_rows(key)
    key = jax.random.fold_in(key, 11)
    keys = jax.random.split(key, 2)
    own_noise = jax.random.normal(keys[0], (BATCH, D), jnp.float32)
    row_scale = jnp.exp(jax.random.uniform(keys[1], (BATCH, 1), jnp.float32, jnp.log(0.5), jnp.log(4.0)))
    return jnp.clip((base + rising_weight(0.25, 1.5) * own_noise) * row_scale / 4.0, -6.0, 6.0)


def draw_view_two(key, part):
    base = shared_rows(key)
    key = jax.random.fold_in(key, 12)
    keys = jax.random.split(key, 2)
    own_noise = jax.random.normal(keys[0], (BATCH, D), jnp.float32)
    row_scale = jnp.exp(jax.random.uniform(keys[1], (BATCH, 1), jnp.float32, jnp.log(0.5), jnp.log(4.0)))
    return jnp.clip((base + rising_weight(0.25, 1.5) * own_noise) * row_scale / 4.0, -6.0, 6.0)


def setup_inputs(seed: int = 0) -> dict:
    streams_of = jax.random.split(jax.random.key(seed), 3)
    view_one = draw_view_one(jax.random.fold_in(streams_of[2], 71), 0)
    view_two = draw_view_two(jax.random.fold_in(streams_of[2], 71), 0)
    return dict(view_one=view_one, view_two=view_two)


logit_sharpness = 0.2

def reference(view_one, view_two):
    all_rows = view_one.shape[0]
    feature_dim = view_one.shape[1]
    norm_one = jnp.sqrt(lax.optimization_barrier(jnp.sum(view_one * view_one, axis=1, keepdims=True)))
    unit_one = view_one / norm_one
    norm_two = jnp.sqrt(lax.optimization_barrier(jnp.sum(view_two * view_two, axis=1, keepdims=True)))
    unit_two = view_two / norm_two
    source_unit_vectors = unit_one.astype(jnp.bfloat16)
    target_unit_vectors = unit_two.astype(jnp.bfloat16)
    block_rows = min(2048, all_rows)
    block_count = all_rows // block_rows
    right_blocks = target_unit_vectors.reshape(block_count, block_rows, feature_dim)

    def forward(state_pair, tile_share):
        partition_function_sums, matched_exp_terms = state_pair
        cosine_logit_matrix = jnp.dot(source_unit_vectors, tile_share.T, preferred_element_type=jnp.float32) / logit_sharpness
        weights = jnp.exp(cosine_logit_matrix)
        partition_function_sums = partition_function_sums + lax.optimization_barrier(jnp.sum(weights, axis=1))
        matched_exp_terms = matched_exp_terms + jnp.dot(weights.astype(jnp.bfloat16), tile_share, preferred_element_type=jnp.float32)
        return ((partition_function_sums, matched_exp_terms), None)
    start_pair = (jnp.zeros((all_rows,), jnp.float32), jnp.zeros((all_rows, feature_dim), jnp.float32))
    (partition_function_sums, matched_exp_terms), _ = lax.scan(forward, start_pair, right_blocks)
    matched_pair_logits = lax.optimization_barrier(jnp.sum(source_unit_vectors.astype(jnp.float32) * target_unit_vectors.astype(jnp.float32), axis=1)) / logit_sharpness
    loss = jnp.sum(jnp.log(partition_function_sums) - matched_pair_logits) / all_rows
    logit_scale_factor = 1.0 / partition_function_sums
    denominator_flip = logit_scale_factor.astype(jnp.bfloat16)

    def backward(tile_share):
        cosine_logit_matrix = jnp.dot(tile_share, source_unit_vectors.T, preferred_element_type=jnp.float32) / logit_sharpness
        weights = (jnp.exp(cosine_logit_matrix) * denominator_flip.astype(jnp.float32)[None, :]).astype(jnp.bfloat16)
        return jnp.dot(weights, source_unit_vectors, preferred_element_type=jnp.float32)
    target_slot = lax.map(backward, right_blocks).reshape(all_rows, feature_dim)
    source_embedding_grad = (matched_exp_terms * logit_scale_factor[:, None] - target_unit_vectors.astype(jnp.float32)) / logit_sharpness
    target_embedding_grad = (target_slot - source_unit_vectors.astype(jnp.float32)) / logit_sharpness
    grad_one = (source_embedding_grad - unit_one * lax.optimization_barrier(jnp.sum(unit_one * source_embedding_grad, axis=1, keepdims=True))) / norm_one
    grad_two = (target_embedding_grad - unit_two * lax.optimization_barrier(jnp.sum(unit_two * target_embedding_grad, axis=1, keepdims=True))) / norm_two
    return (loss, grad_one, grad_two)
```

```python
import functools

import jax
import jax.numpy as jnp
from jax import lax
from jax.experimental import pallas as pl
from jax.experimental.pallas import tpu as pltpu
from jax.sharding import PartitionSpec as P

MESH = pl.DeviceIdType.MESH
F32, BF16 = jnp.float32, jnp.bfloat16
SHARP = 5.0
EXP2_SCALE = 5.0 * 1.4426950408889634
B = 256
ORDER = (0, 4, 2, 1, 6, 3, 5, 7)
PLACE = {k: p for p, k in enumerate(ORDER)}
FAR = (7, 3, 5, 6, 4, 2, 1)
NEAR = (4, 2, 1)
HOP2 = ((2, 4), (1, 2), (4, 1))
HOP3 = ((3, 4, 0, 96), (5, 2, 96, 80), (6, 1, 176, 80))
A, BB = 0, 1


def position():
    g, i = lax.axis_index("grp"), lax.axis_index("in")
    return g // 2, 2 * (g % 2) + i // 8, (i // 2) % 4, i % 2


def flip_a(v):
    return v + 1 - 2 * (v % 2)


def flip_b(v):
    return (v + 3 + 2 * (v % 2)) % 4


def peer(group, k):
    x, y, z, c = position()
    flip = flip_b if group else flip_a
    x = flip(x) if k & 4 else x
    y = flip(y) if k & 2 else y
    z = flip(z) if k & 1 else z
    return (2 * x + y // 2, 8 * (y % 2) + 2 * z + c)


def sibling():
    return (lax.axis_index("grp"), flip_a(lax.axis_index("in")))


def rows(p, n=1):
    return pl.ds(p * B, n * B)


def nt(a, b):
    return lax.dot_general(a, b, (((1,), (1,)), ((), ())), preferred_element_type=F32)


def tn(a, b):
    return lax.dot_general(a, b, (((0,), (0,)), ((), ())), preferred_element_type=F32)


def nn(a, b):
    return lax.dot_general(a, b, (((1,), (0,)), ((), ())), preferred_element_type=F32)


def tree(parts):
    for bit in (1, 2, 4):
        parts = {k: parts[k] + parts[k ^ bit] for k in parts if not k & bit}
    return parts[0]


def kernel(
    one_ref, two_ref, loss_ref, g1_ref, g2_ref,
    left, right, weights, t8,
    tmine, tsib, tpair, tall,
    nsib_out, nsib_in, n_out, n_in, n_own,
    c_out, c_in, c_own,
    l_pair_out, l_pair_in, l_a_out, l_a_in, l_b_out, l_b_in,
    ss, rs,
):
    counter = [0]
    started = []

    def send(src, dst, device):
        n = counter[0]
        counter[0] += 1
        copy = pltpu.make_async_remote_copy(
            src_ref=src, dst_ref=dst, send_sem=ss.at[n], recv_sem=rs.at[n],
            device_id=device, device_id_type=MESH,
        )
        copy.start()
        started.append(copy)
        return copy

    barrier = pltpu.get_barrier_semaphore()
    pl.semaphore_signal(barrier, 1, device_id=sibling(), device_id_type=MESH)
    for k in FAR:
        for group in (A, BB):
            pl.semaphore_signal(barrier, 1, device_id=peer(group, k), device_id_type=MESH)

    one, two = one_ref[...], two_ref[...]
    norm_one = jnp.sqrt(jnp.sum(one * one, axis=1, keepdims=True))
    norm_two = jnp.sqrt(jnp.sum(two * two, axis=1, keepdims=True))
    left[rows(0), :] = (one / norm_one).astype(BF16)
    right[rows(0), :] = (two / norm_two).astype(BF16)
    pl.semaphore_wait(barrier, 15)

    bufs = (left, right)
    stride = (2, 1)

    def block(group, k, first=0, n=B):
        return bufs[group].at[pl.ds(stride[group] * PLACE[k] * B + first, n)]

    def to_sibling(k):
        return send(left.at[rows(2 * PLACE[k])], left.at[rows(2 * PLACE[k] + 1)], sibling())

    got, side = {}, {}
    for d in NEAR:
        for group in (BB, A):
            got[group, d] = send(block(group, 0), block(group, d), peer(group, d))
    side[0] = to_sibling(0)
    for frm, via in HOP2:
        for group in (BB, A):
            got[group, frm].wait_recv()
            got[group, frm | via] = send(block(group, frm), block(group, frm | via), peer(group, via))
        side[frm] = to_sibling(frm)

    def score(l0, l1, j0, j1):
        n = (j1 - j0) * B
        for lb in range(l0, l1):
            lanes = rows(lb)
            w = jnp.exp2(nt(right[rows(j0, j1 - j0), :], left[lanes, :]) * EXP2_SCALE)
            part = jnp.sum(w.reshape(n // 8, 8, B), axis=0)
            if j0 == 0:
                t8[:, lanes] = part
            else:
                t8[:, lanes] += part
            weights[rows(j0, j1 - j0), lanes] = w.astype(BF16)

    for k in (0, *NEAR):
        side[k].wait_recv()
    score(0, 8, 0, 4)
    last = {}
    for frm, via, first, n in HOP3:
        for group in (BB, A):
            got[group, frm].wait_recv()
            last[group, via] = send(block(group, frm, first, n), block(group, 7, first, n), peer(group, via))
        side[frm] = to_sibling(frm)
    for frm, *_ in HOP3:
        side[frm].wait_recv()
    score(8, 14, 0, 7)
    score(0, 8, 4, 7)
    for copy in last.values():
        copy.wait_recv()
    side[7] = to_sibling(7)
    score(0, 14, 7, 8)
    side[7].wait_recv()
    score(14, 16, 0, 8)

    tmine[...] = jnp.sum(t8[...], axis=0, keepdims=True)
    pair = send(tmine, tsib, sibling())

    def numer(p):
        return tn(weights[:, rows(p)], right[...])

    nsib = {}
    for n, k in enumerate((*FAR, 0)):
        nsib_out[PLACE[k]] = numer(2 * PLACE[k] + 1).astype(BF16)
        nsib[k] = send(nsib_out.at[PLACE[k]], nsib_in.at[PLACE[k]], sibling())
        if n == 0:
            pair.wait_recv()
            other = tsib[...]
            tpair[...] = tmine[...] + jnp.concatenate(
                [other[:, (p ^ 1) * B : (p ^ 1) * B + B] for p in range(16)], axis=1
            )
            tcopies = [send(tpair, tall.at[k], peer(A, k)) for k in FAR]
    ncopies = []
    for k in FAR:
        nsib[k].wait_recv()
        n_out[PLACE[k]] = (numer(2 * PLACE[k]) + nsib_in[PLACE[k]].astype(F32)).astype(BF16)
        ncopies.append(send(n_out.at[PLACE[k]], n_in.at[k], peer(A, k)))
    nsib[0].wait_recv()
    n_own[...] = numer(0) + nsib_in[0].astype(F32)
    for copy in tcopies:
        copy.wait_recv()

    def their_totals(k):
        if k == 0:
            return tpair[...]
        theirs = tall[k]
        places = [2 * PLACE[m ^ k] + c for m in ORDER for c in (0, 1)]
        return jnp.concatenate([theirs[:, p * B : p * B + B] for p in places], axis=1)

    totals = tree({k: their_totals(k) for k in range(8)})
    recip = 1.0 / totals
    recip_row = recip.astype(BF16)

    ccopies = []
    for k in FAR:
        part = nn(weights[rows(PLACE[k]), :] * recip_row, left[...])
        c_out[PLACE[k]] = part.astype(BF16)
        ccopies.append(send(c_out.at[PLACE[k]], c_in.at[k], peer(BB, k)))
    c_own[...] = nn(weights[rows(0), :] * recip_row, left[...])

    mine = jnp.sum(jnp.log(totals[:, :B]), axis=1, keepdims=True)
    unit_l, unit_r = left[rows(0), :].astype(F32), right[rows(0), :].astype(F32)
    dots = jnp.sum(jnp.sum(unit_l * unit_r, axis=1, keepdims=True), axis=0, keepdims=True)
    l_pair_out[...] = jnp.broadcast_to(mine - dots * SHARP, (8, 128))
    copy = send(l_pair_out, l_pair_in, sibling())
    copy.wait_recv()
    l_a_out[...] = l_pair_out[...] + l_pair_in[...]
    copies = [send(l_a_out, l_a_in.at[k], peer(A, k)) for k in FAR]
    for copy in copies:
        copy.wait_recv()
    l_b_out[...] = tree({k: l_a_in[k] if k else l_a_out[...] for k in range(8)})
    copies = [send(l_b_out, l_b_in.at[k], peer(BB, k)) for k in FAR]
    for copy in copies:
        copy.wait_recv()
    loss_ref[...] = tree({k: l_b_in[k] if k else l_b_out[...] for k in range(8)}) * (1.0 / (128 * B))

    def finish(x, grad, out):
        norm = jnp.sqrt(jnp.sum(x * x, axis=1, keepdims=True))
        unit = x / norm
        out[...] = (grad - unit * jnp.sum(unit * grad, axis=1, keepdims=True)) / norm

    scale = jnp.transpose(jnp.broadcast_to(recip[:, :B], (128, B)))
    scale = jnp.concatenate([scale, scale], axis=1)
    total = n_own[...]
    for copy, k in zip(ncopies, FAR):
        copy.wait_recv()
        total = total + n_in[k].astype(F32)
    finish(one_ref[...], (total * scale - right[rows(0), :].astype(F32)) * SHARP, g1_ref)
    total = c_own[...]
    for copy, k in zip(ccopies, FAR):
        copy.wait_recv()
        total = total + c_in[k].astype(F32)
    finish(two_ref[...], (total - left[rows(0), :].astype(F32)) * SHARP, g2_ref)
    for copy in started:
        copy.wait_send()


def step(one, two):
    vmem = pl.BlockSpec(memory_space=pltpu.VMEM)
    blocks = pltpu.VMEM((8, B, B), BF16)
    tile = pltpu.VMEM((8, 128), F32)
    tiles = pltpu.VMEM((8, 8, 128), F32)
    row = pltpu.VMEM((1, 16 * B), F32)
    copies = 2 * 9 + 8 + 8 + 15 + 7 + 15
    loss, g1, g2 = pl.pallas_call(
        kernel,
        out_shape=(
            jax.ShapeDtypeStruct((8, 128), F32),
            jax.ShapeDtypeStruct((B, B), F32),
            jax.ShapeDtypeStruct((B, B), F32),
        ),
        in_specs=[vmem] * 2,
        out_specs=(vmem,) * 3,
        scratch_shapes=[
            pltpu.VMEM((16 * B, B), BF16),
            pltpu.VMEM((8 * B, B), BF16),
            pltpu.VMEM((8 * B, 16 * B), BF16),
            pltpu.VMEM((8, 16 * B), F32),
            row, row, row, pltpu.VMEM((8, 1, 16 * B), F32),
            blocks, blocks, blocks, blocks, pltpu.VMEM((B, B), F32),
            blocks, blocks, pltpu.VMEM((B, B), F32),
            tile, tile, tile, tiles, tile, tiles,
            pltpu.SemaphoreType.DMA((copies,)),
            pltpu.SemaphoreType.DMA((copies,)),
        ],
        compiler_params=pltpu.CompilerParams(
            collective_id=1, has_side_effects=True, vmem_limit_bytes=56 * 2**20
        ),
    )(one, two)
    return loss[0, 0], g1, g2


def solution(mesh):
    return jax.shard_map(
        step,
        mesh=mesh,
        in_specs=(P(("grp", "in"), None), P(("grp", "in"), None)),
        out_specs=(P(), P(("grp", "in"), None), P(("grp", "in"), None)),
        check_vma=False,
    )
```

```python
import functools

import jax
import jax.numpy as jnp
from jax import lax
from jax.experimental import pallas as pl
from jax.experimental.pallas import tpu as pltpu
from jax.sharding import PartitionSpec as P

MESH = pl.DeviceIdType.MESH
F32, BF16 = jnp.float32, jnp.bfloat16
SHARP = 5.0
EXP2_SCALE = 5.0 * 1.4426950408889634
B = 256
ORDER = (0, 4, 2, 1, 6, 3, 5, 7)
PLACE = {k: p for p, k in enumerate(ORDER)}
FAR = (7, 3, 5, 6, 4, 2, 1)
NEAR = (4, 2, 1)
HOP2 = ((2, 4), (1, 2), (4, 1))
HOP3 = ((3, 4, 0, 96), (5, 2, 96, 80), (6, 1, 176, 80))
A, BB = 0, 1


def position():
    g, i = lax.axis_index("grp"), lax.axis_index("in")
    return g // 2, 2 * (g % 2) + i // 8, (i // 2) % 4, i % 2


def flip_a(v):
    return v + 1 - 2 * (v % 2)


def flip_b(v):
    return (v + 3 + 2 * (v % 2)) % 4


def peer(group, k):
    x, y, z, c = position()
    flip = flip_b if group else flip_a
    x = flip(x) if k & 4 else x
    y = flip(y) if k & 2 else y
    z = flip(z) if k & 1 else z
    return (2 * x + y // 2, 8 * (y % 2) + 2 * z + c)


def sibling():
    return (lax.axis_index("grp"), flip_a(lax.axis_index("in")))


def rows(p, n=1):
    return pl.ds(p * B, n * B)


def nt(a, b):
    return lax.dot_general(a, b, (((1,), (1,)), ((), ())), preferred_element_type=F32)


def tn(a, b):
    return lax.dot_general(a, b, (((0,), (0,)), ((), ())), preferred_element_type=F32)


def nn(a, b):
    return lax.dot_general(a, b, (((1,), (0,)), ((), ())), preferred_element_type=F32)


def tree(parts):
    for bit in (1, 2, 4):
        parts = {k: parts[k] + parts[k ^ bit] for k in parts if not k & bit}
    return parts[0]


def kernel(
    one_ref, two_ref, loss_ref, g1_ref, g2_ref,
    left, right, weights, t8,
    tmine, tsib, tpair, tall,
    nsib_out, nsib_in, n_out, n_in, n_own,
    c_out, c_in, c_own,
    l_pair_out, l_pair_in, l_a_out, l_a_in, l_b_out, l_b_in,
    ss, rs,
):
    counter = [0]
    started = []

    def send(src, dst, device):
        n = counter[0]
        counter[0] += 1
        copy = pltpu.make_async_remote_copy(
            src_ref=src, dst_ref=dst, send_sem=ss.at[n], recv_sem=rs.at[n],
            device_id=device, device_id_type=MESH,
        )
        copy.start()
        started.append(copy)
        return copy

    barrier = pltpu.get_barrier_semaphore()
    pl.semaphore_signal(barrier, 1, device_id=sibling(), device_id_type=MESH)
    for k in NEAR:
        for group in (A, BB):
            pl.semaphore_signal(barrier, 1, device_id=peer(group, k), device_id_type=MESH)

    one, two = one_ref[...], two_ref[...]
    norm_one = jnp.sqrt(jnp.sum(one * one, axis=1, keepdims=True))
    norm_two = jnp.sqrt(jnp.sum(two * two, axis=1, keepdims=True))
    left[rows(0), :] = (one / norm_one).astype(BF16)
    right[rows(0), :] = (two / norm_two).astype(BF16)
    pl.semaphore_wait(barrier, 7)

    bufs = (left, right)
    stride = (2, 1)

    def block(group, k, first=0, n=B):
        return bufs[group].at[pl.ds(stride[group] * PLACE[k] * B + first, n)]

    def to_sibling(k):
        return send(left.at[rows(2 * PLACE[k])], left.at[rows(2 * PLACE[k] + 1)], sibling())

    got, side = {}, {}
    for d in NEAR:
        for group in (BB, A):
            got[group, d] = send(block(group, 0), block(group, d), peer(group, d))
    side[0] = to_sibling(0)
    for frm, via in HOP2:
        for group in (BB, A):
            got[group, frm].wait_recv()
            got[group, frm | via] = send(block(group, frm), block(group, frm | via), peer(group, via))
        side[frm] = to_sibling(frm)

    def score(l0, l1, j0, j1):
        n = (j1 - j0) * B
        for lb in range(l0, l1):
            lanes = rows(lb)
            w = jnp.exp2(nt(right[rows(j0, j1 - j0), :], left[lanes, :]) * EXP2_SCALE)
            part = jnp.sum(w.reshape(n // 8, 8, B), axis=0)
            if j0 == 0:
                t8[:, lanes] = part
            else:
                t8[:, lanes] += part
            weights[rows(j0, j1 - j0), lanes] = w.astype(BF16)

    for k in (0, *NEAR):
        side[k].wait_recv()
    score(0, 8, 0, 4)
    last = {}
    for frm, via, first, n in HOP3:
        for group in (BB, A):
            got[group, frm].wait_recv()
            last[group, via] = send(block(group, frm, first, n), block(group, 7, first, n), peer(group, via))
        side[frm] = to_sibling(frm)
    for frm, *_ in HOP3:
        side[frm].wait_recv()
    score(8, 14, 0, 7)
    score(0, 8, 4, 7)
    for copy in last.values():
        copy.wait_recv()
    side[7] = to_sibling(7)
    score(0, 14, 7, 8)
    side[7].wait_recv()
    score(14, 16, 0, 8)

    tmine[...] = jnp.sum(t8[...], axis=0, keepdims=True)
    pair = send(tmine, tsib, sibling())

    def numer(places, core):
        return [tn(weights[:, rows(2 * p + core)], right[...]) for p in places]

    def for_sibling(places):
        for p, part in zip(places, numer(places, 1)):
            nsib_out[p] = part.astype(BF16)
        span = pl.ds(places[0], len(places))
        return send(nsib_out.at[span], nsib_in.at[span], sibling())

    def for_members(places, arrival):
        parts = numer(places, 0)
        arrival.wait_recv()
        for p, part in zip(places, parts):
            part = part + nsib_in[p].astype(F32)
            if p == 0:
                n_own[...] = part
            else:
                n_out[p] = part.astype(BF16)
        for p in reversed(places):
            if p:
                ncopies[p] = send(n_out.at[p], n_in.at[ORDER[p]], peer(A, ORDER[p]))

    def column(places):
        span = rows(places[0], len(places))
        part = nn(weights[span, :] * recip_row, left[...])
        for n, p in enumerate(places):
            if p == 0:
                c_own[...] = part[:B]
            else:
                c_out[p] = part[n * B : n * B + B].astype(BF16)
        for p in reversed(places):
            if p:
                ccopies[p] = send(c_out.at[p], c_in.at[ORDER[p]], peer(BB, ORDER[p]))

    ncopies, ccopies = {}, {}
    near, far = (0, 1, 2, 3), (4, 5, 6, 7)
    far_sib = for_sibling(far)
    pair.wait_recv()
    other = tsib[...]
    tpair[...] = tmine[...] + jnp.concatenate(
        [other[:, (p ^ 1) * B : (p ^ 1) * B + B] for p in range(16)], axis=1
    )
    tcopies = [send(tpair, tall.at[k], peer(A, k)) for k in FAR]
    near_sib = for_sibling(near)
    for_members(far, far_sib)
    for copy in tcopies:
        copy.wait_recv()

    def their_totals(k):
        if k == 0:
            return tpair[...]
        theirs = tall[k]
        places = [2 * PLACE[m ^ k] + c for m in ORDER for c in (0, 1)]
        return jnp.concatenate([theirs[:, p * B : p * B + B] for p in places], axis=1)

    totals = tree({k: their_totals(k) for k in range(8)})
    recip = 1.0 / totals
    recip_row = recip.astype(BF16)

    column(far)
    for_members(near, near_sib)
    column(near)

    mine = jnp.sum(jnp.log(totals[:, :B]), axis=1, keepdims=True)
    unit_l, unit_r = left[rows(0), :].astype(F32), right[rows(0), :].astype(F32)
    dots = jnp.sum(jnp.sum(unit_l * unit_r, axis=1, keepdims=True), axis=0, keepdims=True)
    l_pair_out[...] = jnp.broadcast_to(mine - dots * SHARP, (8, 128))
    copy = send(l_pair_out, l_pair_in, sibling())
    copy.wait_recv()
    l_a_out[...] = l_pair_out[...] + l_pair_in[...]
    copies = [send(l_a_out, l_a_in.at[k], peer(A, k)) for k in FAR]
    for copy in copies:
        copy.wait_recv()
    l_b_out[...] = tree({k: l_a_in[k] if k else l_a_out[...] for k in range(8)})
    copies = [send(l_b_out, l_b_in.at[k], peer(BB, k)) for k in FAR]
    for copy in copies:
        copy.wait_recv()
    loss_ref[...] = tree({k: l_b_in[k] if k else l_b_out[...] for k in range(8)}) * (1.0 / (128 * B))

    scale = jnp.transpose(jnp.broadcast_to(recip[:, :B], (128, B)))
    scale = jnp.concatenate([scale, scale], axis=1)
    total = n_own[...]
    for p in reversed(range(1, 8)):
        ncopies[p].wait_recv()
        total = total + n_in[ORDER[p]].astype(F32)
    g1_ref[...] = (total * scale - right[rows(0), :].astype(F32)) * SHARP
    total = c_own[...]
    for p in reversed(range(1, 8)):
        ccopies[p].wait_recv()
        total = total + c_in[ORDER[p]].astype(F32)
    g2_ref[...] = (total - left[rows(0), :].astype(F32)) * SHARP
    for copy in started:
        copy.wait_send()


def finish_kernel(one_ref, two_ref, loss_ref, g1_ref, g2_ref, out_loss, out_one, out_two):
    for x, grad, out in ((one_ref[...], g1_ref[...], out_one), (two_ref[...], g2_ref[...], out_two)):
        norm = jnp.sqrt(jnp.sum(x * x, axis=1, keepdims=True))
        unit = x / norm
        out[...] = (grad - unit * jnp.sum(unit * grad, axis=1, keepdims=True)) / norm
    out_loss[...] = loss_ref[0:1, 0:1]


def step(one, two):
    vmem = pl.BlockSpec(memory_space=pltpu.VMEM)
    blocks = pltpu.VMEM((8, B, B), BF16)
    tile = pltpu.VMEM((8, 128), F32)
    tiles = pltpu.VMEM((8, 8, 128), F32)
    row = pltpu.VMEM((1, 16 * B), F32)
    copies = 2 * 9 + 8 + 8 + 2 + 7 + 7 + 15
    loss, g1, g2 = pl.pallas_call(
        kernel,
        out_shape=(
            jax.ShapeDtypeStruct((8, 128), F32),
            jax.ShapeDtypeStruct((B, B), F32),
            jax.ShapeDtypeStruct((B, B), F32),
        ),
        in_specs=[vmem] * 2,
        out_specs=(vmem,) * 3,
        scratch_shapes=[
            pltpu.VMEM((16 * B, B), BF16),
            pltpu.VMEM((8 * B, B), BF16),
            pltpu.VMEM((8 * B, 16 * B), BF16),
            pltpu.VMEM((8, 16 * B), F32),
            row, row, row, pltpu.VMEM((8, 1, 16 * B), F32),
            blocks, blocks, blocks, blocks, pltpu.VMEM((B, B), F32),
            blocks, blocks, pltpu.VMEM((B, B), F32),
            tile, tile, tile, tiles, tile, tiles,
            pltpu.SemaphoreType.DMA((copies,)),
            pltpu.SemaphoreType.DMA((copies,)),
        ],
        compiler_params=pltpu.CompilerParams(
            collective_id=1, has_side_effects=True, vmem_limit_bytes=56 * 2**20
        ),
    )(one, two)
    loss, g1, g2 = pl.pallas_call(
        finish_kernel,
        out_shape=(
            jax.ShapeDtypeStruct((1, 1), F32),
            jax.ShapeDtypeStruct((B, B), F32),
            jax.ShapeDtypeStruct((B, B), F32),
        ),
        in_specs=[vmem] * 5,
        out_specs=(vmem,) * 3,
    )(one, two, loss, g1, g2)
    return loss.reshape(()), g1, g2


def solution(mesh):
    return jax.shard_map(
        step,
        mesh=mesh,
        in_specs=(P(("grp", "in"), None), P(("grp", "in"), None)),
        out_specs=(P(), P(("grp", "in"), None), P(("grp", "in"), None)),
        check_vma=False,
    )
```

```python
import functools

import jax
import jax.numpy as jnp
from jax import lax
from jax.experimental import pallas as pl
from jax.experimental.pallas import tpu as pltpu
from jax.sharding import PartitionSpec as P

MESH = pl.DeviceIdType.MESH
F32, BF16 = jnp.float32, jnp.bfloat16
SHARP = 5.0
EXP2_SCALE = 5.0 * 1.4426950408889634
B = 256
ORDER = (0, 4, 2, 1, 6, 3, 5, 7)
PLACE = {k: p for p, k in enumerate(ORDER)}
FAR = (7, 3, 5, 6, 4, 2, 1)
NEAR = (4, 2, 1)
HOP2 = ((2, 4), (1, 2), (4, 1))
HOP3 = ((3, 4, 0, 96), (5, 2, 96, 80), (6, 1, 176, 80))
FIRST = ((6, 4, 2), (3, 2, 1), (5, 1, 4))
CORNER = ((3, 4, 0, 96), (5, 2, 96, 80), (6, 1, 176, 80))
HALF = B // 2
A, BB = 0, 1


def position():
    g, i = lax.axis_index("grp"), lax.axis_index("in")
    return g // 2, 2 * (g % 2) + i // 8, (i // 2) % 4, i % 2


def flip_a(v):
    return v + 1 - 2 * (v % 2)


def flip_b(v):
    return (v + 3 + 2 * (v % 2)) % 4


def peer(group, k):
    x, y, z, c = position()
    flip = flip_b if group else flip_a
    x = flip(x) if k & 4 else x
    y = flip(y) if k & 2 else y
    z = flip(z) if k & 1 else z
    return (2 * x + y // 2, 8 * (y % 2) + 2 * z + c)


def sibling():
    return (lax.axis_index("grp"), flip_a(lax.axis_index("in")))


def rows(p, n=1):
    return pl.ds(p * B, n * B)


def nt(a, b):
    return lax.dot_general(a, b, (((1,), (1,)), ((), ())), preferred_element_type=F32)


def tn(a, b):
    return lax.dot_general(a, b, (((0,), (0,)), ((), ())), preferred_element_type=F32)


def nn(a, b):
    return lax.dot_general(a, b, (((1,), (0,)), ((), ())), preferred_element_type=F32)


def tree(parts):
    for bit in (1, 2, 4):
        parts = {k: parts[k] + parts[k ^ bit] for k in parts if not k & bit}
    return parts[0]


def kernel(
    one_ref, two_ref, loss_ref, g1_ref, g2_ref,
    left, right, weights, t8,
    tmine, tsib, tpair, tall,
    nsib_out, nsib_in, n_out, n_mid, n_corner, n_last, n_acc,
    c_out, c_mid, c_corner, c_last, c_acc,
    recip_ref, l_out, l_in,
    ss, rs,
):
    counter = [0]
    started = []

    def send(src, dst, device):
        n = counter[0]
        counter[0] += 1
        copy = pltpu.make_async_remote_copy(
            src_ref=src, dst_ref=dst, send_sem=ss.at[n], recv_sem=rs.at[n],
            device_id=device, device_id_type=MESH,
        )
        copy.start()
        started.append(copy)
        return copy

    barrier = pltpu.get_barrier_semaphore()
    pl.semaphore_signal(barrier, 1, device_id=sibling(), device_id_type=MESH)
    for k in NEAR:
        for group in (A, BB):
            pl.semaphore_signal(barrier, 1, device_id=peer(group, k), device_id_type=MESH)

    one, two = one_ref[...], two_ref[...]
    norm_one = jnp.sqrt(jnp.sum(one * one, axis=1, keepdims=True))
    norm_two = jnp.sqrt(jnp.sum(two * two, axis=1, keepdims=True))
    left[rows(0), :] = (one / norm_one).astype(BF16)
    right[rows(0), :] = (two / norm_two).astype(BF16)
    pl.semaphore_wait(barrier, 7)

    bufs = (left, right)
    stride = (2, 1)

    def block(group, k, first=0, n=B):
        return bufs[group].at[pl.ds(stride[group] * PLACE[k] * B + first, n)]

    def to_sibling(k):
        return send(left.at[rows(2 * PLACE[k])], left.at[rows(2 * PLACE[k] + 1)], sibling())

    got, side = {}, {}
    for d in NEAR:
        for group in (BB, A):
            got[group, d] = send(block(group, 0), block(group, d), peer(group, d))
    side[0] = to_sibling(0)
    for frm, via in HOP2:
        for group in (BB, A):
            got[group, frm].wait_recv()
            got[group, frm | via] = send(block(group, frm), block(group, frm | via), peer(group, via))
        side[frm] = to_sibling(frm)

    def score(l0, l1, j0, j1):
        n = (j1 - j0) * B
        for lb in range(l0, l1):
            lanes = rows(lb)
            w = jnp.exp2(nt(right[rows(j0, j1 - j0), :], left[lanes, :]) * EXP2_SCALE)
            part = jnp.sum(w.reshape(n // 8, 8, B), axis=0)
            if j0 == 0:
                t8[:, lanes] = part
            else:
                t8[:, lanes] += part
            weights[rows(j0, j1 - j0), lanes] = w.astype(BF16)

    for k in (0, *NEAR):
        side[k].wait_recv()
    score(0, 8, 0, 4)
    last = {}
    for frm, via, first, n in HOP3:
        for group in (BB, A):
            got[group, frm].wait_recv()
            last[group, via] = send(block(group, frm, first, n), block(group, 7, first, n), peer(group, via))
        side[frm] = to_sibling(frm)
    score(0, 8, 4, 7)
    for frm, *_ in HOP3:
        side[frm].wait_recv()
    score(8, 14, 0, 7)
    for copy in last.values():
        copy.wait_recv()
    side[7] = to_sibling(7)
    score(0, 14, 7, 8)
    side[7].wait_recv()
    score(14, 16, 0, 8)
    unit_l, unit_r = left[rows(0), :].astype(F32), right[rows(0), :].astype(F32)
    dots = jnp.sum(jnp.sum(unit_l * unit_r, axis=1, keepdims=True), axis=0, keepdims=True)
    for p in range(16):
        tmine[p : p + 1, :] = jnp.sum(t8[:, rows(p)], axis=0, keepdims=True)
    tmine[16:24, :] = jnp.broadcast_to(dots, (8, B))
    pair = send(tmine, tsib, sibling())

    def numer(places, core):
        return [tn(weights[:, rows(2 * p + core)], right[...]) for p in places]

    def for_sibling(places):
        for p, part in zip(places, numer(places, 1)):
            nsib_out[p] = part.astype(BF16)
        span = pl.ds(places[0], len(places))
        return send(nsib_out.at[span], nsib_in.at[span], sibling())

    def for_members(places, arrival):
        parts = numer(places, 0)
        arrival.wait_recv()
        for p, part in zip(places, parts):
            part = part + nsib_in[p].astype(F32)
            if p < 4:
                n_acc[p] = part
            else:
                n_out[p] = part.astype(BF16)

    def column(places):
        span = rows(places[0], len(places))
        part = nn(weights[span, :] * recip_ref[...].astype(BF16), left[...])
        for n, p in enumerate(places):
            if p < 4:
                c_acc[p] = part[n * B : n * B + B]
            else:
                c_out[p] = part[n * B : n * B + B].astype(BF16)

    def first_stage(group, out, mid, corner):
        copies = {}
        for k, _, first, n in CORNER:
            span = pl.ds(first, n)
            copies[k] = send(out.at[PLACE[7], span], corner.at[span], peer(group, k))
        for h in range(2):
            span = pl.ds(h * HALF, HALF)
            for k, via, to in FIRST:
                copies[to, h] = send(out.at[PLACE[k], span], mid.at[PLACE[to], span], peer(group, via))
        return copies

    def second_stage(group, copies, acc, out, mid, corner, last):
        done = {}
        for k, to, first, n in CORNER:
            copies[k].wait_recv()
            span = pl.ds(first, n)
            acc[PLACE[to], span] += corner[span].astype(F32)
        for h in range(2):
            span = pl.ds(h * HALF, HALF)
            for _, _, to in FIRST:
                copies[to, h].wait_recv()
            for _, _, to in FIRST:
                p = PLACE[to]
                out[p, span] = (acc[p, span] + mid[p, span].astype(F32)).astype(BF16)
                done[to, h] = send(out.at[p, span], last.at[p, span], peer(group, to))
        return done

    def whole(copies, acc, last):
        for copy in copies.values():
            copy.wait_recv()
        return (acc[0] + last[1].astype(F32)) + (last[2].astype(F32) + last[3].astype(F32))

    near, far = (0, 1, 2, 3), (4, 5, 6, 7)
    far_sib = for_sibling(far)
    pair.wait_recv()
    for p in range(16):
        tpair[p : p + 1, :] = tmine[p : p + 1, :] + tsib[(p ^ 1) : (p ^ 1) + 1, :]
    tpair[16:24, :] = tmine[16:24, :] + tsib[16:24, :]
    tcopies = [send(tpair, tall.at[k], peer(A, k)) for k in FAR]
    near_sib = for_sibling(near)
    for_members(far, far_sib)
    n_copies = first_stage(A, n_out, n_mid, n_corner)
    for copy in tcopies:
        copy.wait_recv()

    def total_row(m, c):
        parts = {}
        for k in range(8):
            p = 2 * PLACE[m ^ k] + c
            parts[k] = tall[k, p : p + 1, :] if k else tpair[p : p + 1, :]
        return tree(parts)

    logs = {}
    for m in range(8):
        both = [total_row(m, c) for c in range(2)]
        for c in range(2):
            recip_ref[:, rows(2 * PLACE[m] + c)] = 1.0 / both[c]
        logs[m] = jnp.log(both[0]) + jnp.log(both[1])
    diagonals = tree({k: tall[k, 16:17, :] if k else tpair[16:17, :] for k in range(8)})
    cube = jnp.sum(tree(logs), axis=1, keepdims=True) - diagonals[:, :1] * SHARP
    l_out[...] = jnp.broadcast_to(cube, (8, 128))
    lcopies = [send(l_out, l_in.at[k], peer(BB, k)) for k in FAR]

    column(far)
    c_copies = first_stage(BB, c_out, c_mid, c_corner)
    for_members(near, near_sib)
    column(near)
    n_copies = second_stage(A, n_copies, n_acc, n_out, n_mid, n_corner, n_last)
    c_copies = second_stage(BB, c_copies, c_acc, c_out, c_mid, c_corner, c_last)

    scale = jnp.transpose(jnp.broadcast_to(recip_ref[:, :B], (128, B)))
    scale = jnp.concatenate([scale, scale], axis=1)
    total = whole(n_copies, n_acc, n_last)
    g1_ref[...] = (total * scale - right[rows(0), :].astype(F32)) * SHARP
    total = whole(c_copies, c_acc, c_last)
    g2_ref[...] = (total - left[rows(0), :].astype(F32)) * SHARP
    for copy in lcopies:
        copy.wait_recv()
    loss_ref[...] = tree({k: l_in[k] if k else l_out[...] for k in range(8)}) * (1.0 / (128 * B))
    for copy in started:
        copy.wait_send()


def finish_kernel(one_ref, two_ref, loss_ref, g1_ref, g2_ref, out_loss, out_one, out_two):
    for x, grad, out in ((one_ref[...], g1_ref[...], out_one), (two_ref[...], g2_ref[...], out_two)):
        norm = jnp.sqrt(jnp.sum(x * x, axis=1, keepdims=True))
        unit = x / norm
        out[...] = (grad - unit * jnp.sum(unit * grad, axis=1, keepdims=True)) / norm
    out_loss[...] = loss_ref[0:1, 0:1]


def step(one, two):
    vmem = pl.BlockSpec(memory_space=pltpu.VMEM)
    blocks = lambda n: pltpu.VMEM((n, B, B), BF16)
    parts = [blocks(8), blocks(4), pltpu.VMEM((B, B), BF16), blocks(4), pltpu.VMEM((4, B, B), F32)]
    tile = pltpu.VMEM((8, 128), F32)
    tiles = pltpu.VMEM((8, 8, 128), F32)
    table = pltpu.VMEM((24, B), F32)
    copies = 2 * 9 + 8 + 8 + 2 + 7 + 2 * 15
    loss, g1, g2 = pl.pallas_call(
        kernel,
        out_shape=(
            jax.ShapeDtypeStruct((8, 128), F32),
            jax.ShapeDtypeStruct((B, B), F32),
            jax.ShapeDtypeStruct((B, B), F32),
        ),
        in_specs=[vmem] * 2,
        out_specs=(vmem,) * 3,
        scratch_shapes=[
            pltpu.VMEM((16 * B, B), BF16),
            pltpu.VMEM((8 * B, B), BF16),
            pltpu.VMEM((8 * B, 16 * B), BF16),
            pltpu.VMEM((8, 16 * B), F32),
            table, table, table, pltpu.VMEM((8, 24, B), F32),
            blocks(8), blocks(8), *parts, *parts,
            pltpu.VMEM((1, 16 * B), F32), tile, tiles,
            pltpu.SemaphoreType.DMA((copies,)),
            pltpu.SemaphoreType.DMA((copies,)),
        ],
        compiler_params=pltpu.CompilerParams(
            collective_id=1, has_side_effects=True, vmem_limit_bytes=56 * 2**20
        ),
    )(one, two)
    loss, g1, g2 = pl.pallas_call(
        finish_kernel,
        out_shape=(
            jax.ShapeDtypeStruct((1, 1), F32),
            jax.ShapeDtypeStruct((B, B), F32),
            jax.ShapeDtypeStruct((B, B), F32),
        ),
        in_specs=[vmem] * 5,
        out_specs=(vmem,) * 3,
    )(one, two, loss, g1, g2)
    return loss.reshape(()), g1, g2


def solution(mesh):
    return jax.shard_map(
        step,
        mesh=mesh,
        in_specs=(P(("grp", "in"), None), P(("grp", "in"), None)),
        out_specs=(P(), P(("grp", "in"), None), P(("grp", "in"), None)),
        check_vma=False,
    )
```

```python
import functools

import jax
import jax.numpy as jnp
from jax import lax
from jax.experimental import pallas as pl
from jax.experimental.pallas import tpu as pltpu
from jax.sharding import PartitionSpec as P

MESH = pl.DeviceIdType.MESH
F32, BF16 = jnp.float32, jnp.bfloat16
SHARP = 5.0
EXP2_SCALE = 5.0 * 1.4426950408889634
B = 256
ORDER = (0, 4, 2, 1, 6, 3, 5, 7)
PLACE = {k: p for p, k in enumerate(ORDER)}
FAR = (7, 3, 5, 6, 4, 2, 1)
NEAR = (4, 2, 1)
HOP2 = ((2, 4), (1, 2), (4, 1))
HOP3 = ((3, 4, 0, 96), (5, 2, 96, 80), (6, 1, 176, 80))
FIRST = ((6, 4, 2), (3, 2, 1), (5, 1, 4))
CORNER = ((3, 4, 0, 96), (5, 2, 96, 80), (6, 1, 176, 80))
HALF = B // 2
EXTRA = pl.ds(16 * B, 128)
A, BB = 0, 1


def position():
    g, i = lax.axis_index("grp"), lax.axis_index("in")
    return g // 2, 2 * (g % 2) + i // 8, (i // 2) % 4, i % 2


def flip_a(v):
    return v + 1 - 2 * (v % 2)


def flip_b(v):
    return (v + 3 + 2 * (v % 2)) % 4


def peer(group, k):
    x, y, z, c = position()
    flip = flip_b if group else flip_a
    x = flip(x) if k & 4 else x
    y = flip(y) if k & 2 else y
    z = flip(z) if k & 1 else z
    return (2 * x + y // 2, 8 * (y % 2) + 2 * z + c)


def sibling():
    return (lax.axis_index("grp"), flip_a(lax.axis_index("in")))


def rows(p, n=1):
    return pl.ds(p * B, n * B)


def nt(a, b):
    return lax.dot_general(a, b, (((1,), (1,)), ((), ())), preferred_element_type=F32)


def tn(a, b):
    return lax.dot_general(a, b, (((0,), (0,)), ((), ())), preferred_element_type=F32)


def nn(a, b):
    return lax.dot_general(a, b, (((1,), (0,)), ((), ())), preferred_element_type=F32)


def tree(parts):
    for bit in (1, 2, 4):
        parts = {k: parts[k] + parts[k ^ bit] for k in parts if not k & bit}
    return parts[0]


def kernel(
    one_ref, two_ref, loss_ref, g1_ref, g2_ref,
    left, right, weights, t8,
    tmine, tsib, tpair, tall,
    nsib_out, nsib_in, n_out, n_mid, n_corner, n_last, n_acc,
    c_out, c_mid, c_corner, c_last, c_acc,
    recip_ref, l_out, l_in,
    ss, rs,
):
    counter = [0]
    started = []

    def send(src, dst, device):
        n = counter[0]
        counter[0] += 1
        copy = pltpu.make_async_remote_copy(
            src_ref=src, dst_ref=dst, send_sem=ss.at[n], recv_sem=rs.at[n],
            device_id=device, device_id_type=MESH,
        )
        copy.start()
        started.append(copy)
        return copy

    barrier = pltpu.get_barrier_semaphore()
    pl.semaphore_signal(barrier, 1, device_id=sibling(), device_id_type=MESH)
    for k in NEAR:
        for group in (A, BB):
            pl.semaphore_signal(barrier, 1, device_id=peer(group, k), device_id_type=MESH)

    def unit_rows(ref):
        x = ref[...]
        return (x / jnp.sqrt(jnp.sum(x * x, axis=1, keepdims=True))).astype(BF16)

    right[rows(0), :] = unit_rows(two_ref)
    left[rows(0), :] = unit_rows(one_ref)
    pl.semaphore_wait(barrier, 7)

    bufs = (left, right)
    stride = (2, 1)

    def block(group, k, first=0, n=B):
        return bufs[group].at[pl.ds(stride[group] * PLACE[k] * B + first, n)]

    def to_sibling(k):
        return send(left.at[rows(2 * PLACE[k])], left.at[rows(2 * PLACE[k] + 1)], sibling())

    got, side = {}, {}
    for d in NEAR:
        got[BB, d] = send(block(BB, 0), block(BB, d), peer(BB, d))
    for d in NEAR:
        got[A, d] = send(block(A, 0), block(A, d), peer(A, d))
    side[0] = to_sibling(0)
    for frm, via in HOP2:
        for group in (BB, A):
            got[group, frm].wait_recv()
            got[group, frm | via] = send(block(group, frm), block(group, frm | via), peer(group, via))
        side[frm] = to_sibling(frm)

    def score(l0, l1, j0, j1):
        n = (j1 - j0) * B
        for lb in range(l0, l1):
            lanes = rows(lb)
            w = jnp.exp2(nt(right[rows(j0, j1 - j0), :], left[lanes, :]) * EXP2_SCALE)
            part = jnp.sum(w.reshape(n // 8, 8, B), axis=0)
            if j0 == 0:
                t8[:, lanes] = part
            else:
                t8[:, lanes] += part
            weights[rows(j0, j1 - j0), lanes] = w.astype(BF16)

    for k in (0, *NEAR):
        side[k].wait_recv()
    score(0, 8, 0, 4)
    last = {}
    for frm, via, first, n in HOP3:
        for group in (BB, A):
            got[group, frm].wait_recv()
            last[group, via] = send(block(group, frm, first, n), block(group, 7, first, n), peer(group, via))
        side[frm] = to_sibling(frm)
    score(0, 8, 4, 7)
    for frm, *_ in HOP3:
        side[frm].wait_recv()
    score(8, 14, 0, 7)
    for copy in last.values():
        copy.wait_recv()
    side[7] = to_sibling(7)
    score(0, 14, 7, 8)
    side[7].wait_recv()
    score(14, 16, 0, 8)
    unit_l, unit_r = left[rows(0), :].astype(F32), right[rows(0), :].astype(F32)
    dots = jnp.sum(jnp.sum(unit_l * unit_r, axis=1, keepdims=True), axis=0, keepdims=True)
    for p in range(16):
        tmine[:, rows(p)] = jnp.sum(t8[:, rows(p)], axis=0, keepdims=True)
    tmine[:, EXTRA] = jnp.broadcast_to(dots, (1, 128))
    pair = send(tmine, tsib, sibling())

    def numer(places, core):
        return [tn(weights[:, rows(2 * p + core)], right[...]) for p in places]

    def for_sibling(places):
        for p, part in zip(places, numer(places, 1)):
            nsib_out[p] = part.astype(BF16)
        span = pl.ds(places[0], len(places))
        return send(nsib_out.at[span], nsib_in.at[span], sibling())

    def for_members(places, arrival):
        parts = numer(places, 0)
        arrival.wait_recv()
        for p, part in zip(places, parts):
            part = part + nsib_in[p].astype(F32)
            if p < 4:
                n_acc[p] = part
            else:
                n_out[p] = part.astype(BF16)

    def column(places):
        scale = recip_ref[...].astype(BF16)
        for p in places:
            part = nn(weights[rows(p), :] * scale, left[...])
            if p < 4:
                c_acc[p] = part
            else:
                c_out[p] = part.astype(BF16)

    def first_stage(group, out, mid, corner, members):
        copies = {}
        for k, _, first, n in CORNER if 7 in members else ():
            span = pl.ds(first, n)
            copies[k] = send(out.at[PLACE[7], span], corner.at[span], peer(group, k))
        for h in range(2):
            span = pl.ds(h * HALF, HALF)
            for k, via, to in FIRST:
                if k in members:
                    copies[to, h] = send(out.at[PLACE[k], span], mid.at[PLACE[to], span], peer(group, via))
        return copies

    def second_stage(group, copies, acc, out, mid, corner, last):
        done = {}
        for k, to, first, n in CORNER:
            copies[k].wait_recv()
            span = pl.ds(first, n)
            acc[PLACE[to], span] += corner[span].astype(F32)
        for h in range(2):
            span = pl.ds(h * HALF, HALF)
            for _, _, to in FIRST:
                copies[to, h].wait_recv()
            for _, _, to in FIRST:
                p = PLACE[to]
                out[p, span] = (acc[p, span] + mid[p, span].astype(F32)).astype(BF16)
                done[to, h] = send(out.at[p, span], last.at[p, span], peer(group, to))
        return done

    def whole(copies, acc, last):
        for copy in copies.values():
            copy.wait_recv()
        return (acc[0] + last[1].astype(F32)) + (last[2].astype(F32) + last[3].astype(F32))

    near, far = (0, 1, 2, 3), (4, 5, 6, 7)
    far_sib = for_sibling(far)
    pair.wait_recv()
    for p in range(16):
        tpair[:, rows(p)] = tmine[:, rows(p)] + tsib[:, rows(p ^ 1)]
    tpair[:, EXTRA] = tmine[:, EXTRA] + tsib[:, EXTRA]
    tcopies = [send(tpair, tall.at[k], peer(A, k)) for k in FAR]
    near_sib = for_sibling(near)
    for_members(far, far_sib)
    n_copies = first_stage(A, n_out, n_mid, n_corner, FAR[:4])
    for copy in tcopies:
        copy.wait_recv()

    def total_row(m, c):
        parts = {}
        for k in range(8):
            p = 2 * PLACE[m ^ k] + c
            parts[k] = tall[k, :, rows(p)] if k else tpair[:, rows(p)]
        return tree(parts)

    logs = {}
    for m in range(8):
        both = [total_row(m, c) for c in range(2)]
        for c in range(2):
            recip_ref[:, rows(2 * PLACE[m] + c)] = 1.0 / both[c]
        logs[m] = jnp.log(both[0]) + jnp.log(both[1])
    diagonals = tree({k: tall[k, :, EXTRA] if k else tpair[:, EXTRA] for k in range(8)})
    cube = jnp.sum(tree(logs), axis=1, keepdims=True) - diagonals[:, :1] * SHARP
    l_out[...] = jnp.broadcast_to(cube, (8, 128))
    lcopies = [send(l_out, l_in.at[k], peer(BB, k)) for k in FAR]

    c_copies = {}
    for places in ((7, 6), (5, 4)):
        column(places)
        c_copies |= first_stage(BB, c_out, c_mid, c_corner, [ORDER[p] for p in places])
    for_members(near, near_sib)
    column(near)
    n_copies = second_stage(A, n_copies, n_acc, n_out, n_mid, n_corner, n_last)
    c_copies = second_stage(BB, c_copies, c_acc, c_out, c_mid, c_corner, c_last)

    scale = jnp.transpose(jnp.broadcast_to(recip_ref[:, :B], (128, B)))
    scale = jnp.concatenate([scale, scale], axis=1)
    total = whole(n_copies, n_acc, n_last)
    g1_ref[...] = (total * scale - right[rows(0), :].astype(F32)) * SHARP
    total = whole(c_copies, c_acc, c_last)
    g2_ref[...] = (total - left[rows(0), :].astype(F32)) * SHARP
    for copy in lcopies:
        copy.wait_recv()
    loss_ref[...] = tree({k: l_in[k] if k else l_out[...] for k in range(8)}) * (1.0 / (128 * B))
    for copy in started:
        copy.wait_send()


def finish_kernel(one_ref, two_ref, loss_ref, g1_ref, g2_ref, out_loss, out_one, out_two):
    for x, grad, out in ((one_ref[...], g1_ref[...], out_one), (two_ref[...], g2_ref[...], out_two)):
        norm = jnp.sqrt(jnp.sum(x * x, axis=1, keepdims=True))
        unit = x / norm
        out[...] = (grad - unit * jnp.sum(unit * grad, axis=1, keepdims=True)) / norm
    out_loss[...] = loss_ref[0:1, 0:1]


def step(one, two):
    vmem = pl.BlockSpec(memory_space=pltpu.VMEM)
    blocks = lambda n: pltpu.VMEM((n, B, B), BF16)
    parts = [blocks(8), blocks(4), pltpu.VMEM((B, B), BF16), blocks(4), pltpu.VMEM((4, B, B), F32)]
    tile = pltpu.VMEM((8, 128), F32)
    tiles = pltpu.VMEM((8, 8, 128), F32)
    table = pltpu.VMEM((1, 16 * B + 128), F32)
    copies = 2 * 9 + 8 + 8 + 2 + 7 + 2 * 15
    loss, g1, g2 = pl.pallas_call(
        kernel,
        out_shape=(
            jax.ShapeDtypeStruct((8, 128), F32),
            jax.ShapeDtypeStruct((B, B), F32),
            jax.ShapeDtypeStruct((B, B), F32),
        ),
        in_specs=[vmem] * 2,
        out_specs=(vmem,) * 3,
        scratch_shapes=[
            pltpu.VMEM((16 * B, B), BF16),
            pltpu.VMEM((8 * B, B), BF16),
            pltpu.VMEM((8 * B, 16 * B), BF16),
            pltpu.VMEM((8, 16 * B), F32),
            table, table, table, pltpu.VMEM((8, 1, 16 * B + 128), F32),
            blocks(8), blocks(8), *parts, *parts,
            pltpu.VMEM((1, 16 * B), F32), tile, tiles,
            pltpu.SemaphoreType.DMA((copies,)),
            pltpu.SemaphoreType.DMA((copies,)),
        ],
        compiler_params=pltpu.CompilerParams(
            collective_id=1, has_side_effects=True, vmem_limit_bytes=56 * 2**20
        ),
    )(one, two)
    loss, g1, g2 = pl.pallas_call(
        finish_kernel,
        out_shape=(
            jax.ShapeDtypeStruct((1, 1), F32),
            jax.ShapeDtypeStruct((B, B), F32),
            jax.ShapeDtypeStruct((B, B), F32),
        ),
        in_specs=[vmem] * 5,
        out_specs=(vmem,) * 3,
    )(one, two, loss, g1, g2)
    return loss.reshape(()), g1, g2


def solution(mesh):
    return jax.shard_map(
        step,
        mesh=mesh,
        in_specs=(P(("grp", "in"), None), P(("grp", "in"), None)),
        out_specs=(P(), P(("grp", "in"), None), P(("grp", "in"), None)),
        check_vma=False,
    )
```

```python
import functools

import jax
import jax.numpy as jnp
from jax import lax
from jax.experimental import pallas as pl
from jax.experimental.pallas import tpu as pltpu
from jax.sharding import PartitionSpec as P

MESH = pl.DeviceIdType.MESH
F32, BF16 = jnp.float32, jnp.bfloat16
SHARP = 5.0
EXP2_SCALE = 5.0 * 1.4426950408889634
B = 256
ORDER = (0, 4, 2, 1, 6, 3, 5, 7)
PLACE = {k: p for p, k in enumerate(ORDER)}
FAR = (7, 3, 5, 6, 4, 2, 1)
NEAR = (4, 2, 1)
HOP2 = ((2, 4), (1, 2), (4, 1))
HOP3 = ((3, 4, 0, 96), (5, 2, 96, 80), (6, 1, 176, 80))
FIRST = ((6, 4, 2), (3, 2, 1), (5, 1, 4))
CORNER = ((3, 4, 0, 96), (5, 2, 96, 80), (6, 1, 176, 80))
HALF = B // 2
EXTRA = pl.ds(16 * B, 128)
A, BB = 0, 1


def position():
    g, i = lax.axis_index("grp"), lax.axis_index("in")
    return g // 2, 2 * (g % 2) + i // 8, (i // 2) % 4, i % 2


def flip_a(v):
    return v + 1 - 2 * (v % 2)


def flip_b(v):
    return (v + 3 + 2 * (v % 2)) % 4


def peer(group, k):
    x, y, z, c = position()
    flip = flip_b if group else flip_a
    x = flip(x) if k & 4 else x
    y = flip(y) if k & 2 else y
    z = flip(z) if k & 1 else z
    return (2 * x + y // 2, 8 * (y % 2) + 2 * z + c)


def sibling():
    return (lax.axis_index("grp"), flip_a(lax.axis_index("in")))


def rows(p, n=1):
    return pl.ds(p * B, n * B)


def nt(a, b):
    return lax.dot_general(a, b, (((1,), (1,)), ((), ())), preferred_element_type=F32)


def tn(a, b):
    return lax.dot_general(a, b, (((0,), (0,)), ((), ())), preferred_element_type=F32)


def nn(a, b):
    return lax.dot_general(a, b, (((1,), (0,)), ((), ())), preferred_element_type=F32)


def tree(parts):
    for bit in (1, 2, 4):
        parts = {k: parts[k] + parts[k ^ bit] for k in parts if not k & bit}
    return parts[0]


def kernel(
    one_ref, two_ref, loss_ref, g1_ref, g2_ref,
    left, right, weights, t8,
    tmine, tsib, tpair, tall,
    nsib_out, nsib_in, n_out, n_mid, n_corner, n_last, n_acc,
    c_out, c_mid, c_corner, c_last, c_acc,
    recip_ref, l_out, l_in,
    ss, rs,
):
    counter = [0]
    started = []

    def send(src, dst, device):
        n = counter[0]
        counter[0] += 1
        copy = pltpu.make_async_remote_copy(
            src_ref=src, dst_ref=dst, send_sem=ss.at[n], recv_sem=rs.at[n],
            device_id=device, device_id_type=MESH,
        )
        copy.start()
        started.append(copy)
        return copy

    barrier = pltpu.get_barrier_semaphore()
    pl.semaphore_signal(barrier, 1, device_id=sibling(), device_id_type=MESH)
    for k in NEAR:
        for group in (A, BB):
            pl.semaphore_signal(barrier, 1, device_id=peer(group, k), device_id_type=MESH)

    def unit_rows(ref):
        x = ref[...]
        return (x / jnp.sqrt(jnp.sum(x * x, axis=1, keepdims=True))).astype(BF16)

    right[rows(0), :] = unit_rows(two_ref)
    left[rows(0), :] = unit_rows(one_ref)
    pl.semaphore_wait(barrier, 7)

    bufs = (left, right)
    stride = (2, 1)

    def block(group, k, first=0, n=B):
        return bufs[group].at[pl.ds(stride[group] * PLACE[k] * B + first, n)]

    def to_sibling(k):
        return send(left.at[rows(2 * PLACE[k])], left.at[rows(2 * PLACE[k] + 1)], sibling())

    got, side = {}, {}
    for d in NEAR:
        got[BB, d] = send(block(BB, 0), block(BB, d), peer(BB, d))
    for d in NEAR:
        got[A, d] = send(block(A, 0), block(A, d), peer(A, d))
    side[0] = to_sibling(0)
    for frm, via in HOP2:
        for group in (BB, A):
            got[group, frm].wait_recv()
            got[group, frm | via] = send(block(group, frm), block(group, frm | via), peer(group, via))
        side[frm] = to_sibling(frm)

    def score(blocks, j0, j1):
        n = (j1 - j0) * B
        for lb in blocks:
            lanes = rows(lb)
            w = jnp.exp2(nt(right[rows(j0, j1 - j0), :], left[lanes, :]) * EXP2_SCALE)
            part = jnp.sum(w.reshape(n // 8, 8, B), axis=0)
            if j0 == 0:
                t8[:, lanes] = part
            else:
                t8[:, lanes] += part
            weights[rows(j0, j1 - j0), lanes] = w.astype(BF16)

    score((0, 2, 4, 6), 0, 4)
    for k in (0, *NEAR):
        side[k].wait_recv()
    score((1, 3, 5, 7), 0, 4)
    last = {}
    for frm, via, first, n in HOP3:
        for group in (BB, A):
            got[group, frm].wait_recv()
            last[group, via] = send(block(group, frm, first, n), block(group, 7, first, n), peer(group, via))
        side[frm] = to_sibling(frm)
    score(range(8), 4, 7)
    score((8, 10, 12), 0, 7)
    for frm, *_ in HOP3:
        side[frm].wait_recv()
    score((9, 11, 13), 0, 7)
    for copy in last.values():
        copy.wait_recv()
    side[7] = to_sibling(7)
    score(range(14), 7, 8)
    score((14,), 0, 8)
    side[7].wait_recv()
    score((15,), 0, 8)
    unit_l, unit_r = left[rows(0), :].astype(F32), right[rows(0), :].astype(F32)
    dots = jnp.sum(jnp.sum(unit_l * unit_r, axis=1, keepdims=True), axis=0, keepdims=True)
    for p in range(16):
        tmine[:, rows(p)] = jnp.sum(t8[:, rows(p)], axis=0, keepdims=True)
    tmine[:, EXTRA] = jnp.broadcast_to(dots, (1, 128))
    pair = send(tmine, tsib, sibling())

    def numer(places, core):
        return [tn(weights[:, rows(2 * p + core)], right[...]) for p in places]

    def for_sibling(places):
        for p, part in zip(places, numer(places, 1)):
            nsib_out[p] = part.astype(BF16)
        span = pl.ds(places[0], len(places))
        return send(nsib_out.at[span], nsib_in.at[span], sibling())

    def for_members(places, arrival):
        parts = numer(places, 0)
        arrival.wait_recv()
        for p, part in zip(places, parts):
            part = part + nsib_in[p].astype(F32)
            if p < 4:
                n_acc[p] = part
            else:
                n_out[p] = part.astype(BF16)

    def column(places):
        scale = recip_ref[...].astype(BF16)
        for p in places:
            part = nn(weights[rows(p), :] * scale, left[...])
            if p < 4:
                c_acc[p] = part
            else:
                c_out[p] = part.astype(BF16)

    def first_stage(group, out, mid, corner, members):
        copies = {}
        for k, _, first, n in CORNER if 7 in members else ():
            span = pl.ds(first, n)
            copies[k] = send(out.at[PLACE[7], span], corner.at[span], peer(group, k))
        for h in range(2):
            span = pl.ds(h * HALF, HALF)
            for k, via, to in FIRST:
                if k in members:
                    copies[to, h] = send(out.at[PLACE[k], span], mid.at[PLACE[to], span], peer(group, via))
        return copies

    def second_stage(group, copies, acc, out, mid, corner, last):
        done = {}
        for k, to, first, n in CORNER:
            copies[k].wait_recv()
            span = pl.ds(first, n)
            acc[PLACE[to], span] += corner[span].astype(F32)
        for h in range(2):
            span = pl.ds(h * HALF, HALF)
            for _, _, to in FIRST:
                copies[to, h].wait_recv()
            for _, _, to in FIRST:
                p = PLACE[to]
                out[p, span] = (acc[p, span] + mid[p, span].astype(F32)).astype(BF16)
                done[to, h] = send(out.at[p, span], last.at[p, span], peer(group, to))
        return done

    def whole(copies, acc, last):
        for copy in copies.values():
            copy.wait_recv()
        return (acc[0] + last[1].astype(F32)) + (last[2].astype(F32) + last[3].astype(F32))

    near, far = (0, 1, 2, 3), (4, 5, 6, 7)
    far_sib = for_sibling(far)
    pair.wait_recv()
    for p in range(16):
        tpair[:, rows(p)] = tmine[:, rows(p)] + tsib[:, rows(p ^ 1)]
    tpair[:, EXTRA] = tmine[:, EXTRA] + tsib[:, EXTRA]
    tcopies = [send(tpair, tall.at[k], peer(A, k)) for k in FAR]
    near_sib = for_sibling(near)
    for_members(far, far_sib)
    n_copies = first_stage(A, n_out, n_mid, n_corner, FAR[:4])
    for copy in tcopies:
        copy.wait_recv()

    def total_row(m, c):
        parts = {}
        for k in range(8):
            p = 2 * PLACE[m ^ k] + c
            parts[k] = tall[k, :, rows(p)] if k else tpair[:, rows(p)]
        return tree(parts)

    totals = {}
    for m in range(8):
        for c in range(2):
            totals[m, c] = total_row(m, c)
            recip_ref[:, rows(2 * PLACE[m] + c)] = 1.0 / totals[m, c]

    c_copies = {}
    for places in ((7, 6), (5, 4)):
        column(places)
        c_copies |= first_stage(BB, c_out, c_mid, c_corner, [ORDER[p] for p in places])
    logs = tree({m: jnp.log(totals[m, 0]) + jnp.log(totals[m, 1]) for m in range(8)})
    diagonals = tree({k: tall[k, :, EXTRA] if k else tpair[:, EXTRA] for k in range(8)})
    cube = jnp.sum(logs, axis=1, keepdims=True) - diagonals[:, :1] * SHARP
    l_out[...] = jnp.broadcast_to(cube, (8, 128))
    lcopies = [send(l_out, l_in.at[k], peer(BB, k)) for k in FAR]
    for_members(near, near_sib)
    column(near)
    n_copies = second_stage(A, n_copies, n_acc, n_out, n_mid, n_corner, n_last)
    c_copies = second_stage(BB, c_copies, c_acc, c_out, c_mid, c_corner, c_last)

    scale = jnp.transpose(jnp.broadcast_to(recip_ref[:, :B], (128, B)))
    scale = jnp.concatenate([scale, scale], axis=1)
    def finish(ref, grad, out):
        x = ref[...]
        norm = jnp.sqrt(jnp.sum(x * x, axis=1, keepdims=True))
        unit = x / norm
        out[...] = (grad - unit * jnp.sum(unit * grad, axis=1, keepdims=True)) / norm

    total = whole(n_copies, n_acc, n_last)
    finish(one_ref, (total * scale - right[rows(0), :].astype(F32)) * SHARP, g1_ref)
    total = whole(c_copies, c_acc, c_last)
    finish(two_ref, (total - left[rows(0), :].astype(F32)) * SHARP, g2_ref)
    for copy in lcopies:
        copy.wait_recv()
    loss_ref[...] = tree({k: l_in[k] if k else l_out[...] for k in range(8)}) * (1.0 / (128 * B))
    for copy in started:
        copy.wait_send()


def hand_over(loss_ref, g1_ref, g2_ref, out_loss, out_one, out_two):
    out_loss[...] = loss_ref[0:1, 0:1]
    out_one[...] = g1_ref[...]
    out_two[...] = g2_ref[...]


def step(one, two):
    vmem = pl.BlockSpec(memory_space=pltpu.VMEM)
    blocks = lambda n: pltpu.VMEM((n, B, B), BF16)
    parts = [blocks(8), blocks(4), pltpu.VMEM((B, B), BF16), blocks(4), pltpu.VMEM((4, B, B), F32)]
    tile = pltpu.VMEM((8, 128), F32)
    tiles = pltpu.VMEM((8, 8, 128), F32)
    table = pltpu.VMEM((1, 16 * B + 128), F32)
    copies = 2 * 9 + 8 + 8 + 2 + 7 + 2 * 15
    loss, g1, g2 = pl.pallas_call(
        kernel,
        out_shape=(
            jax.ShapeDtypeStruct((8, 128), F32),
            jax.ShapeDtypeStruct((B, B), F32),
            jax.ShapeDtypeStruct((B, B), F32),
        ),
        in_specs=[vmem] * 2,
        out_specs=(vmem,) * 3,
        scratch_shapes=[
            pltpu.VMEM((16 * B, B), BF16),
            pltpu.VMEM((8 * B, B), BF16),
            pltpu.VMEM((8 * B, 16 * B), BF16),
            pltpu.VMEM((8, 16 * B), F32),
            table, table, table, pltpu.VMEM((8, 1, 16 * B + 128), F32),
            blocks(8), blocks(8), *parts, *parts,
            pltpu.VMEM((1, 16 * B), F32), tile, tiles,
            pltpu.SemaphoreType.DMA((copies,)),
            pltpu.SemaphoreType.DMA((copies,)),
        ],
        compiler_params=pltpu.CompilerParams(
            collective_id=1, has_side_effects=True, vmem_limit_bytes=56 * 2**20
        ),
    )(one, two)
    loss, g1, g2 = pl.pallas_call(
        hand_over,
        out_shape=(
            jax.ShapeDtypeStruct((1, 1), F32),
            jax.ShapeDtypeStruct((B, B), F32),
            jax.ShapeDtypeStruct((B, B), F32),
        ),
        in_specs=[vmem] * 3,
        out_specs=(vmem,) * 3,
    )(loss, g1, g2)
    return loss.reshape(()), g1, g2


def solution(mesh):
    return jax.shard_map(
        step,
        mesh=mesh,
        in_specs=(P(("grp", "in"), None), P(("grp", "in"), None)),
        out_specs=(P(), P(("grp", "in"), None), P(("grp", "in"), None)),
        check_vma=False,
    )
```

```python
import functools

import jax
import jax.numpy as jnp
from jax import lax
from jax.experimental import pallas as pl
from jax.experimental.pallas import tpu as pltpu
from jax.sharding import PartitionSpec as P

MESH = pl.DeviceIdType.MESH
F32, BF16 = jnp.float32, jnp.bfloat16
SHARP = 5.0
EXP2_SCALE = 5.0 * 1.4426950408889634
B = 256
ORDER = (0, 4, 2, 1, 6, 3, 5, 7)
PLACE = {k: p for p, k in enumerate(ORDER)}
FAR = (7, 3, 5, 6, 4, 2, 1)
NEAR = (4, 2, 1)
HOP2 = ((2, 4), (1, 2), (4, 1))
HOP3 = ((3, 4, 0, 96), (5, 2, 96, 80), (6, 1, 176, 80))
FIRST = ((6, 4, 2), (3, 2, 1), (5, 1, 4))
CORNER = ((3, 4, 0, 96), (5, 2, 96, 80), (6, 1, 176, 80))
HALF = B // 2
EXTRA = pl.ds(16 * B, 128)
A, BB = 0, 1


def position():
    g, i = lax.axis_index("grp"), lax.axis_index("in")
    return g // 2, 2 * (g % 2) + i // 8, (i // 2) % 4, i % 2


def flip_a(v):
    return v + 1 - 2 * (v % 2)


def flip_b(v):
    return (v + 3 + 2 * (v % 2)) % 4


def peer(group, k):
    x, y, z, c = position()
    flip = flip_b if group else flip_a
    x = flip(x) if k & 4 else x
    y = flip(y) if k & 2 else y
    z = flip(z) if k & 1 else z
    return (2 * x + y // 2, 8 * (y % 2) + 2 * z + c)


def sibling():
    return (lax.axis_index("grp"), flip_a(lax.axis_index("in")))


def rows(p, n=1):
    return pl.ds(p * B, n * B)


def nt(a, b):
    return lax.dot_general(a, b, (((1,), (1,)), ((), ())), preferred_element_type=F32)


def tn(a, b):
    return lax.dot_general(a, b, (((0,), (0,)), ((), ())), preferred_element_type=F32)


def nn(a, b):
    return lax.dot_general(a, b, (((1,), (0,)), ((), ())), preferred_element_type=F32)


def tree(parts):
    for bit in (1, 2, 4):
        parts = {k: parts[k] + parts[k ^ bit] for k in parts if not k & bit}
    return parts[0]


def kernel(
    one_hbm, two_hbm, loss_ref, g1_ref, g2_ref,
    one_ref, two_ref, in_sem,
    left, right, weights, t8,
    tmine, tsib, tpair, tall,
    nsib_out, nsib_in, n_out, n_mid, n_corner, n_last, n_acc,
    c_out, c_mid, c_corner, c_last, c_acc,
    recip_ref, l_out, l_in,
    ss, rs,
):
    counter = [0]
    started = []

    def send(src, dst, device):
        n = counter[0]
        counter[0] += 1
        copy = pltpu.make_async_remote_copy(
            src_ref=src, dst_ref=dst, send_sem=ss.at[n], recv_sem=rs.at[n],
            device_id=device, device_id_type=MESH,
        )
        copy.start()
        started.append(copy)
        return copy

    load_two = pltpu.make_async_copy(two_hbm, two_ref, in_sem.at[0])
    load_one = pltpu.make_async_copy(one_hbm, one_ref, in_sem.at[1])
    load_two.start()
    load_one.start()
    barrier = pltpu.get_barrier_semaphore()
    pl.semaphore_signal(barrier, 1, device_id=sibling(), device_id_type=MESH)
    for k in NEAR:
        for group in (A, BB):
            pl.semaphore_signal(barrier, 1, device_id=peer(group, k), device_id_type=MESH)

    def unit_rows(ref):
        x = ref[...]
        return (x / jnp.sqrt(jnp.sum(x * x, axis=1, keepdims=True))).astype(BF16)

    load_two.wait()
    right[rows(0), :] = unit_rows(two_ref)
    load_one.wait()
    left[rows(0), :] = unit_rows(one_ref)
    pl.semaphore_wait(barrier, 7)

    bufs = (left, right)
    stride = (2, 1)

    def block(group, k, first=0, n=B):
        return bufs[group].at[pl.ds(stride[group] * PLACE[k] * B + first, n)]

    def to_sibling(k):
        return send(left.at[rows(2 * PLACE[k])], left.at[rows(2 * PLACE[k] + 1)], sibling())

    got, side = {}, {}
    for d in NEAR:
        for group in (A, BB):
            got[group, d] = send(block(group, 0), block(group, d), peer(group, d))
    side[0] = to_sibling(0)
    for frm, via in HOP2:
        for group in (A, BB):
            got[group, frm].wait_recv()
            got[group, frm | via] = send(block(group, frm), block(group, frm | via), peer(group, via))
            if group == A:
                side[frm] = to_sibling(frm)

    def score(blocks, j0, j1):
        n = (j1 - j0) * B
        for lb in blocks:
            lanes = rows(lb)
            w = jnp.exp2(nt(right[rows(j0, j1 - j0), :], left[lanes, :]) * EXP2_SCALE)
            part = jnp.sum(w.reshape(n // 8, 8, B), axis=0)
            if j0 == 0:
                t8[:, lanes] = part
            else:
                t8[:, lanes] += part
            weights[rows(j0, j1 - j0), lanes] = w.astype(BF16)

    score((0, 2, 4, 6), 0, 4)
    for k in (0, *NEAR):
        side[k].wait_recv()
    score((1, 3, 5, 7), 0, 4)
    last = {}
    for frm, via, first, n in HOP3:
        for group in (A, BB):
            got[group, frm].wait_recv()
            last[group, via] = send(block(group, frm, first, n), block(group, 7, first, n), peer(group, via))
            if group == A:
                side[frm] = to_sibling(frm)
    score(range(8), 4, 7)
    score((8, 10, 12), 0, 7)
    for frm, *_ in HOP3:
        side[frm].wait_recv()
    score((9, 11, 13), 0, 7)
    for copy in last.values():
        copy.wait_recv()
    side[7] = to_sibling(7)
    score(range(14), 7, 8)
    score((14,), 0, 8)
    side[7].wait_recv()
    score((15,), 0, 8)
    unit_l, unit_r = left[rows(0), :].astype(F32), right[rows(0), :].astype(F32)
    dots = jnp.sum(jnp.sum(unit_l * unit_r, axis=1, keepdims=True), axis=0, keepdims=True)
    for p in range(16):
        tmine[:, rows(p)] = jnp.sum(t8[:, rows(p)], axis=0, keepdims=True)
    tmine[:, EXTRA] = jnp.broadcast_to(dots, (1, 128))
    pair = send(tmine, tsib, sibling())

    def numer(places, core):
        return [tn(weights[:, rows(2 * p + core)], right[...]) for p in places]

    def for_sibling(places):
        for p, part in zip(places, numer(places, 1)):
            nsib_out[p] = part.astype(BF16)
        span = pl.ds(places[0], len(places))
        return send(nsib_out.at[span], nsib_in.at[span], sibling())

    def for_members(places, arrival):
        parts = numer(places, 0)
        arrival.wait_recv()
        for p, part in zip(places, parts):
            part = part + nsib_in[p].astype(F32)
            if p < 4:
                n_acc[p] = part
            else:
                n_out[p] = part.astype(BF16)

    def column(places):
        scale = recip_ref[...].astype(BF16)
        for p in places:
            part = nn(weights[rows(p), :] * scale, left[...])
            if p < 4:
                c_acc[p] = part
            else:
                c_out[p] = part.astype(BF16)

    def first_stage(group, out, mid, corner, members):
        copies = {}
        for k, _, first, n in CORNER if 7 in members else ():
            span = pl.ds(first, n)
            copies[k] = send(out.at[PLACE[7], span], corner.at[span], peer(group, k))
        for h in range(2):
            span = pl.ds(h * HALF, HALF)
            for k, via, to in FIRST:
                if k in members:
                    copies[to, h] = send(out.at[PLACE[k], span], mid.at[PLACE[to], span], peer(group, via))
        return copies

    def second_stage(group, copies, acc, out, mid, corner, last):
        done = {}
        for k, to, first, n in CORNER:
            copies[k].wait_recv()
            span = pl.ds(first, n)
            acc[PLACE[to], span] += corner[span].astype(F32)
        for h in range(2):
            span = pl.ds(h * HALF, HALF)
            for _, _, to in FIRST:
                copies[to, h].wait_recv()
            for _, _, to in FIRST:
                p = PLACE[to]
                out[p, span] = (acc[p, span] + mid[p, span].astype(F32)).astype(BF16)
                done[to, h] = send(out.at[p, span], last.at[p, span], peer(group, to))
        return done

    def whole(copies, acc, last):
        for copy in copies.values():
            copy.wait_recv()
        return (acc[0] + last[1].astype(F32)) + (last[2].astype(F32) + last[3].astype(F32))

    near, far = (0, 1, 2, 3), (4, 5, 6, 7)
    far_sib = for_sibling(far)
    pair.wait_recv()
    for p in range(16):
        tpair[:, rows(p)] = tmine[:, rows(p)] + tsib[:, rows(p ^ 1)]
    tpair[:, EXTRA] = tmine[:, EXTRA] + tsib[:, EXTRA]
    tcopies = [send(tpair, tall.at[k], peer(A, k)) for k in FAR]
    near_sib = for_sibling(near)
    for_members(far, far_sib)
    n_copies = first_stage(A, n_out, n_mid, n_corner, FAR[:4])
    for copy in tcopies:
        copy.wait_recv()

    def total_row(m, c):
        parts = {}
        for k in range(8):
            p = 2 * PLACE[m ^ k] + c
            parts[k] = tall[k, :, rows(p)] if k else tpair[:, rows(p)]
        return tree(parts)

    totals = {}
    for m in range(8):
        for c in range(2):
            totals[m, c] = total_row(m, c)
            recip_ref[:, rows(2 * PLACE[m] + c)] = 1.0 / totals[m, c]

    c_copies = {}
    for places in ((7, 6), (5, 4)):
        column(places)
        c_copies |= first_stage(BB, c_out, c_mid, c_corner, [ORDER[p] for p in places])
    logs = tree({m: jnp.log(totals[m, 0]) + jnp.log(totals[m, 1]) for m in range(8)})
    diagonals = tree({k: tall[k, :, EXTRA] if k else tpair[:, EXTRA] for k in range(8)})
    cube = jnp.sum(logs, axis=1, keepdims=True) - diagonals[:, :1] * SHARP
    l_out[...] = jnp.broadcast_to(cube, (8, 128))
    lcopies = [send(l_out, l_in.at[k], peer(BB, k)) for k in FAR]
    for_members(near, near_sib)
    column(near)
    n_copies = second_stage(A, n_copies, n_acc, n_out, n_mid, n_corner, n_last)
    c_copies = second_stage(BB, c_copies, c_acc, c_out, c_mid, c_corner, c_last)

    scale = jnp.transpose(jnp.broadcast_to(recip_ref[:, :B], (128, B)))
    scale = jnp.concatenate([scale, scale], axis=1)
    def finish(ref, grad, out):
        x = ref[...]
        norm = jnp.sqrt(jnp.sum(x * x, axis=1, keepdims=True))
        unit = x / norm
        out[...] = (grad - unit * jnp.sum(unit * grad, axis=1, keepdims=True)) / norm

    total = whole(n_copies, n_acc, n_last)
    finish(one_ref, (total * scale - right[rows(0), :].astype(F32)) * SHARP, g1_ref)
    total = whole(c_copies, c_acc, c_last)
    finish(two_ref, (total - left[rows(0), :].astype(F32)) * SHARP, g2_ref)
    for copy in lcopies:
        copy.wait_recv()
    loss_ref[...] = tree({k: l_in[k] if k else l_out[...] for k in range(8)}) * (1.0 / (128 * B))
    for copy in started:
        copy.wait_send()


def hand_over(loss_ref, g1_ref, g2_ref, out_loss, out_one, out_two):
    out_loss[...] = loss_ref[0:1, 0:1]
    out_one[...] = g1_ref[...]
    out_two[...] = g2_ref[...]


def step(one, two):
    vmem = pl.BlockSpec(memory_space=pltpu.VMEM)
    blocks = lambda n: pltpu.VMEM((n, B, B), BF16)
    parts = [blocks(8), blocks(4), pltpu.VMEM((B, B), BF16), blocks(4), pltpu.VMEM((4, B, B), F32)]
    tile = pltpu.VMEM((8, 128), F32)
    tiles = pltpu.VMEM((8, 8, 128), F32)
    table = pltpu.VMEM((1, 16 * B + 128), F32)
    copies = 2 * 9 + 8 + 8 + 2 + 7 + 2 * 15
    loss, g1, g2 = pl.pallas_call(
        kernel,
        out_shape=(
            jax.ShapeDtypeStruct((8, 128), F32),
            jax.ShapeDtypeStruct((B, B), F32),
            jax.ShapeDtypeStruct((B, B), F32),
        ),
        in_specs=[pl.BlockSpec(memory_space=pltpu.HBM)] * 2,
        out_specs=(vmem,) * 3,
        scratch_shapes=[
            pltpu.VMEM((B, B), F32),
            pltpu.VMEM((B, B), F32),
            pltpu.SemaphoreType.DMA((2,)),
            pltpu.VMEM((16 * B, B), BF16),
            pltpu.VMEM((8 * B, B), BF16),
            pltpu.VMEM((8 * B, 16 * B), BF16),
            pltpu.VMEM((8, 16 * B), F32),
            table, table, table, pltpu.VMEM((8, 1, 16 * B + 128), F32),
            blocks(8), blocks(8), *parts, *parts,
            pltpu.VMEM((1, 16 * B), F32), tile, tiles,
            pltpu.SemaphoreType.DMA((copies,)),
            pltpu.SemaphoreType.DMA((copies,)),
        ],
        compiler_params=pltpu.CompilerParams(
            collective_id=1, has_side_effects=True, vmem_limit_bytes=56 * 2**20
        ),
    )(one, two)
    loss, g1, g2 = pl.pallas_call(
        hand_over,
        out_shape=(
            jax.ShapeDtypeStruct((1, 1), F32),
            jax.ShapeDtypeStruct((B, B), F32),
            jax.ShapeDtypeStruct((B, B), F32),
        ),
        in_specs=[vmem] * 3,
        out_specs=(vmem,) * 3,
    )(loss, g1, g2)
    return loss.reshape(()), g1, g2


def solution(mesh):
    return jax.shard_map(
        step,
        mesh=mesh,
        in_specs=(P(("grp", "in"), None), P(("grp", "in"), None)),
        out_specs=(P(), P(("grp", "in"), None), P(("grp", "in"), None)),
        check_vma=False,
    )
```
